512 devices in a mesh: group: 8 (over x, y_lo), blk: 64 (over y_hi, z, core).
Axes of the slice: x: 4, y: 8 (y_hi: 4, y_lo: 2; y = y_hi * 2 + y_lo), z: 8, core: 2. Of those that a mesh axis runs over, the one named last changes fastest.
Arguments:
- images: float32 [131072, 1152], P(('group', 'blk')), may hold values from -6 to 6
- texts: float32 [131072, 1152], P(('group', 'blk')), may hold values from -6 to 6
- image_ids: int32 [131072], P(('group', 'blk')), may hold values from 0 to 131071, as said below
- text_ids: int32 [131072], P(('group', 'blk')), may hold values from 0 to 131071, as said below
- log_scale: float32 [1], replicated, may hold values from 1.5 to 2.5
- bias: float32 [1], replicated, may hold values from -3 to -1
Outputs:
- row_loss: float32 [131072], P(('group', 'blk'))
- image_grad: float32 [131072, 1152], P(('group', 'blk'))
- text_grad: float32 [131072, 1152], P(('group', 'blk'))
The draws below stay inside these ranges and needn't reach their ends.
Inputs may be any that keep to these rules, and one draw needn't show every extreme that they name: image_ids is a permutation of 0 to 131071. text_ids is a permutation of 0 to 131071; each text id equals the id of exactly one image, and that image's block meets the text's block in one of the 4 rounds.
All inputs are finite; a program needn't handle non-finite values.
Results may differ from the reference program's by a relative error of at most 0.005.
Values may be sent and summed in bfloat16 or wider, within the bound.
A program may use at most 64 MiB of HBM per device.

```python
import jax
import jax.numpy as jnp
from jax import lax

D = 1152
ROWS = 256
PAIRS = 131072
N_GROUP = 8
N_BLK = 64


def pair_tables(key):
    order = jax.random.permutation(jax.random.fold_in(key, 11), PAIRS).astype(jnp.int32)
    rounds = jax.random.randint(jax.random.fold_in(key, 12), (ROWS,), 0, 4)
    places = jax.random.permutation(jax.random.fold_in(key, 13), ROWS).astype(jnp.int32)
    group_idx = jnp.arange(N_GROUP, dtype=jnp.int32)[:, None, None]
    blk_idx = jnp.arange(N_BLK, dtype=jnp.int32)[None, :, None]
    which = rounds[None, None, :]
    step_blk = jnp.where(which == 1, 1, jnp.where(which == 2, 2, 0))
    step_group = jnp.where(which == 3, 1, 0)
    target_blk = (blk_idx + step_blk) % N_BLK
    target_group = (group_idx + step_group) % N_GROUP
    target_row = (target_group * N_BLK + target_blk) * ROWS + places[None, None, :]
    text_side = order[target_row.reshape(-1)]
    return (order, text_side)


def draw_image_ids(key, part):
    image_side, text_side = pair_tables(key)
    return image_side


def draw_text_ids(key, part):
    image_side, text_side = pair_tables(key)
    return text_side


def steps_of(key, extent, split, least, top_value):
    factor_of, own = 1.0, jax.random.fold_in(key, 6)
    for dim, blocks in split:
        heights = jnp.exp(jax.random.uniform(jax.random.fold_in(own, dim), (blocks,), jnp.float32, least / len(split), top_value / len(split)))
        factor_of = factor_of * jnp.repeat(heights, extent[dim] // blocks).reshape([-1 if axis == dim else 1 for axis in range(len(extent))])
    return factor_of


def normal_values(key, shape, deviation, limit, pieces=(), kind=jnp.bfloat16):
    values = deviation * jax.random.normal(key, shape, jnp.float32)
    if pieces:
        values = values * steps_of(key, shape, pieces, -0.22, 0.18)
    return jnp.clip(values, -limit, limit).astype(kind)


def setup_inputs(seed: int = 0) -> dict:
    keys = jax.random.split(jax.random.key(seed), 7)
    images = normal_values(keys[0], (PAIRS, D), 1.0, 6.0, ((0, 512),), jnp.float32)
    texts = normal_values(keys[1], (PAIRS, D), 1.0, 6.0, ((0, 512),), jnp.float32)
    image_ids = draw_image_ids(jax.random.fold_in(keys[6], 71), 0)
    text_ids = draw_text_ids(jax.random.fold_in(keys[6], 71), 0)
    log_scale = jnp.clip(jax.random.uniform(keys[4], (1,), jnp.float32, 1.5, 2.5), 1.5, 2.5)
    bias = jnp.clip(jax.random.uniform(keys[5], (1,), jnp.float32, -3.0, -1.0), -3.0, -1.0)
    return {"images": images, "texts": texts, "image_ids": image_ids, "text_ids": text_ids, "log_scale": log_scale, "bias": bias}


def normalize(values):
    inverse = lax.rsqrt(lax.optimization_barrier(jnp.sum(values * values, axis=-1, keepdims=True)) + 1e-06)
    return (inverse, values * inverse)

def unit_backward(inverse, unit, grad):
    return inverse * (grad - unit * lax.optimization_barrier(jnp.sum(unit * grad, axis=-1, keepdims=True)))

def reference(images, texts, image_ids, text_ids, log_scale, bias):
    scale = jnp.exp(log_scale[0])
    shift_b = bias[0]
    image_norm, image_unit = normalize(images)
    text_norm, text_unit = normalize(texts)
    image_half = image_unit.astype(jnp.bfloat16).reshape(N_GROUP, N_BLK, ROWS, D)
    text_half = text_unit.astype(jnp.bfloat16).reshape(N_GROUP, N_BLK, ROWS, D)
    img_ids = image_ids.reshape(N_GROUP, N_BLK, ROWS)
    txt_ids = text_ids.reshape(N_GROUP, N_BLK, ROWS)
    img_f = image_half.astype(jnp.float32)
    row_loss = jnp.zeros((N_GROUP, N_BLK, ROWS), jnp.float32)
    image_unit_grad = jnp.zeros((N_GROUP, N_BLK, ROWS, D), jnp.float32)
    text_unit_grad = jnp.zeros((N_GROUP, N_BLK, ROWS, D), jnp.float32)
    moves = [(0, 0), (1, 1), (1, 2), (0, 1)]
    for axis_move, amount in moves:
        met_text = jnp.roll(text_half, amount, axis=axis_move)
        met_ids = jnp.roll(txt_ids, amount, axis=axis_move)
        txt_f = met_text.astype(jnp.float32)
        dots = jnp.einsum('gkid,gkjd->gkij', img_f, txt_f)
        logit = scale * dots + shift_b
        label = jnp.where(img_ids[..., :, None] == met_ids[..., None, :], 1.0, -1.0).astype(jnp.float32)
        row_loss = row_loss + lax.optimization_barrier(jnp.sum(jax.nn.softplus(-label * logit), axis=-1))
        coeff = (-label * scale * jax.nn.sigmoid(-label * logit)).astype(jnp.bfloat16).astype(jnp.float32)
        image_unit_grad = image_unit_grad + jnp.einsum('gkij,gkjd->gkid', coeff, txt_f)
        partial_value = jnp.einsum('gkij,gkid->gkjd', coeff, img_f)
        text_unit_grad = text_unit_grad + jnp.roll(partial_value, -amount, axis=axis_move)
    image_grad = unit_backward(image_norm, image_unit, image_unit_grad.reshape(PAIRS, D))
    text_grad = unit_backward(text_norm, text_unit, text_unit_grad.reshape(PAIRS, D))
    return (row_loss.reshape(PAIRS), image_grad, text_grad)
```

```python
import functools

import jax
import jax.numpy as jnp
from jax import lax
from jax.experimental import pallas as pl
from jax.experimental.pallas import tpu as pltpu
from jax.sharding import PartitionSpec as P

MESH = pl.DeviceIdType.MESH
ROWS = 256
D = 1152
N_Z = 8
N_YHI = 4
N_GROUP = 8
STRIP = ROWS // N_Z
CHUNK = 64
N_CHUNK = ROWS // CHUNK
TILE = 384
F32 = jnp.float32
BF16 = jnp.bfloat16


def rows_of(ref, start, count):
    return ref.at[pl.ds(start, count)]


def kernel(
    images, texts, image_ids, text_ids, log_scale, bias,
    loss_out, image_out, text_out,
    im, tx, ih, th, inv_i, inv_t, acc_i, acc_t, loss_acc, col_i, col_t, ids,
    t1, t2, tg, i1, i2, ig, relay_t, relay_i, ids_in,
    load_sem, send_sem, chunk_send, chunk_recv, block_recv, ids_send, ids_recv, strip_send, ready_next, ready_strip, ready_wrap,
):
    g = lax.axis_index("group")
    k = lax.axis_index("blk")
    core = lax.rem(k, 2)
    z = lax.rem(k // 2, N_Z)
    yhi = k // (2 * N_Z)
    first, last = z == 0, z == N_Z - 1

    def at(yh, zz, cc):
        return (g, (lax.rem(yh + N_YHI, N_YHI) * N_Z + zz) * 2 + cc)

    g_next = (lax.rem(g + 1, N_GROUP), k)
    g_prev = (lax.rem(g + N_GROUP - 1, N_GROUP), k)
    partner = (g, k + 1 - 2 * core)
    wrap_next = at(yhi + 1, 0, core)
    wrap_prev = at(yhi - 1, N_Z - 1, core)
    k_next = (g, lax.rem(k + 2, 2 * N_Z * N_YHI))
    k_prev = (g, lax.rem(k + 2 * N_Z * N_YHI - 2, 2 * N_Z * N_YHI))

    barrier = pltpu.get_barrier_semaphore()

    def tell(device):
        pl.semaphore_signal(barrier, inc=1, device_id=device, device_id_type=MESH)

    tell(g_next)
    tell(g_prev)
    tell(partner)

    loads = []
    for c in range(N_CHUNK):
        for a, (src, dst) in enumerate(((texts, tx), (images, im))):
            rows = pl.ds(c * CHUNK, CHUNK)
            copy = pltpu.make_async_copy(src.at[rows], dst.at[rows], load_sem.at[a, c])
            copy.start()
            loads.append(copy)

    @pl.when(jnp.logical_not(last))
    def _():
        tell(k_next)
        tell(at(yhi, N_Z - 1, core))
        tell(wrap_prev)

    @pl.when(last)
    def _():
        tell(at(yhi + 1, N_Z - 1, core))

    @pl.when(first)
    def _():
        for s in range(N_Z):
            tell(at(yhi - 1, s, core))
        for s in range(1, N_Z):
            tell(at(yhi, s, core))

    ids[...] = jnp.concatenate(
        [text_ids[...], image_ids[...], jnp.zeros((6, ROWS), jnp.int32)], axis=0
    )
    col_t[...] = jnp.broadcast_to(text_ids[...].astype(F32), (128, ROWS)).T
    col_i[...] = jnp.broadcast_to(image_ids[...].astype(F32), (128, ROWS)).T
    scale = jnp.exp(jnp.full((1, 1), log_scale[0], F32))
    offset = bias[0]

    def remote(src, dst, send, recv, device):
        return pltpu.make_async_remote_copy(
            src_ref=src, dst_ref=dst, send_sem=send, recv_sem=recv,
            device_id=device, device_id_type=MESH,
        )

    def group_text(c):
        return remote(rows_of(th, c * CHUNK, CHUNK), rows_of(tg, c * CHUNK, CHUNK),
                      chunk_send.at[0, c], chunk_recv.at[0, c], g_next)

    def group_image(c):
        return remote(rows_of(ih, c * CHUNK, CHUNK), rows_of(ig, c * CHUNK, CHUNK),
                      chunk_send.at[1, c], chunk_recv.at[1, c], g_prev)

    half = ROWS // 2

    def next_text(part):
        return remote(rows_of(th, part * half, half), rows_of(t2, part * half, half),
                      send_sem.at[part], block_recv.at[0], k_next)

    def prev_image(part):
        return remote(rows_of(ih, part * half, half), rows_of(i2, part * half, half),
                      send_sem.at[2 + part], block_recv.at[1], k_prev)

    def strip_text(s):
        return remote(rows_of(th, s * STRIP, STRIP), relay_t, strip_send.at[s], block_recv.at[2], at(yhi, s, core))

    def strip_image(s):
        return remote(rows_of(ih, s * STRIP, STRIP), relay_i, strip_send.at[s], block_recv.at[3], at(yhi, s, core))

    mine = pl.multiple_of(z * STRIP, STRIP)
    pass_text = remote(relay_t, rows_of(t2, mine, STRIP), send_sem.at[4], block_recv.at[0], wrap_next)
    pass_image = remote(relay_i, rows_of(i2, mine, STRIP), send_sem.at[5], block_recv.at[1], wrap_prev)
    end = (N_Z - 1) * STRIP
    own_text = remote(rows_of(th, end, STRIP), rows_of(t2, end, STRIP), send_sem.at[4], block_recv.at[0], wrap_next)
    own_image = remote(rows_of(ih, 0, STRIP), rows_of(i2, 0, STRIP), send_sem.at[5], block_recv.at[1], wrap_prev)

    core_text = remote(th, t1, send_sem.at[6], block_recv.at[4], partner)
    core_image = remote(ih, i1, send_sem.at[6], block_recv.at[5], partner)
    on_text = remote(t2, t1, send_sem.at[7], block_recv.at[4], partner)
    on_image = remote(i2, i1, send_sem.at[7], block_recv.at[5], partner)

    def send_ids(slot, device, src=ids):
        return remote(src, ids_in.at[slot], ids_send.at[slot], ids_recv.at[slot], device)

    ids_next, ids_prev = send_ids(2, k_next), send_ids(3, k_prev)
    ids_copies = [send_ids(0, g_next), send_ids(1, g_prev), send_ids(4, partner)]
    ids_on_text = send_ids(5, partner, ids_in.at[2])
    ids_on_image = send_ids(5, partner, ids_in.at[3])

    def normalize(c, raw, half_ref, inv_ref):
        rows = pl.ds(c * CHUNK, CHUNK)
        values = raw[rows, :]
        inv = lax.rsqrt(jnp.sum(values * values, axis=-1, keepdims=True) + 1e-06)
        half_ref[rows, :] = (values * inv).astype(BF16)
        inv_ref[rows, :] = jnp.broadcast_to(inv, (CHUNK, 128))

    for c in range(N_CHUNK):
        loads[2 * c].wait()
        normalize(c, tx, th, inv_t)
        if c == 0:
            pl.semaphore_wait(
                barrier, 4 + 2 * (z > 0).astype(jnp.int32) + 15 * last.astype(jnp.int32)
            )
        if c < 2:
            group_text(c).start()

        @pl.when(last)
        def _():
            for s in range(c * CHUNK // STRIP, (c + 1) * CHUNK // STRIP):
                if s < N_Z - 1:
                    strip_text(s).start()
                else:
                    own_text.start()

        if c == 0:
            @pl.when(z > 0)
            def _():
                pl.semaphore_signal(ready_next, inc=1, device_id=k_prev, device_id_type=MESH)
                pl.semaphore_signal(ready_strip.at[z], inc=1, device_id=at(yhi, 0, core), device_id_type=MESH)

            @pl.when(last)
            def _():
                for s in range(N_Z - 1):
                    pl.semaphore_signal(ready_wrap, inc=1, device_id=at(yhi + 1, s, core), device_id_type=MESH)

        loads[2 * c + 1].wait()
        normalize(c, im, ih, inv_i)
        if c < 2:
            group_image(c).start()

    for copy in ids_copies:
        copy.start()

    @pl.when(core == 0)
    def _():
        core_text.start()

    @pl.when(core == 1)
    def _():
        core_image.start()

    @pl.when(z > 0)
    def _():
        ids_prev.start()
        prev_image(0).start()
        prev_image(1).start()

    @pl.when(jnp.logical_not(last))
    def _():
        pl.semaphore_wait(ready_next, 1)
        ids_next.start()
        next_text(0).start()

    @pl.when(last)
    def _():
        ids_next.start()

    @pl.when(jnp.logical_not(last) & (z > 0))
    def _():
        next_text(1).start()

    def side(own_half, own_col, other, start, count, other_ids, acc, loss, fresh=False):
        block = other[pl.ds(start, count), :]
        dots = lax.dot_general(
            own_half[...], block, (((1,), (1,)), ((), ())), preferred_element_type=F32
        )
        logit = scale * dots + offset
        same = own_col[:, 0:1] == other_ids.astype(F32)
        u = jnp.where(same, -logit, logit)
        e = jnp.exp(-jnp.abs(u))
        coeff = jnp.where(same, -scale, scale) * (jnp.where(u >= 0, 1.0, e) / (1.0 + e))
        coeff = coeff.astype(BF16)
        if loss is not None:
            terms = jnp.maximum(u, 0.0) + jnp.log1p(e)
            terms = jnp.sum(terms, axis=1, keepdims=True)
            terms = jnp.broadcast_to(terms, (ROWS, 128))
            loss[...] = terms if fresh else loss[...] + terms

        def add(t, carry):
            cols = pl.ds(pl.multiple_of(t * TILE, 128), TILE)
            term = jnp.dot(coeff, other[pl.ds(start, count), cols], preferred_element_type=F32)
            acc[:, cols] = term if fresh else acc[:, cols] + term
            return carry

        lax.fori_loop(0, D // TILE, add, 0)

    def image_side(block, text_row, start=0, count=ROWS, fresh=False):
        side(ih, col_i, block, start, count, text_row, acc_i, loss_acc, fresh)

    def text_side(block, image_row, start=0, count=ROWS, fresh=False):
        side(th, col_t, block, start, count, image_row, acc_t, None, fresh)

    image_side(th, ids[0:1, :], fresh=True)

    @pl.when(first)
    def _():
        for s in range(1, 5):
            pl.semaphore_wait(ready_strip.at[s], 1)
            strip_image(s).start()
        next_text(1).start()

    text_side(ih, ids[1:2, :], fresh=True)

    send_ids(4, partner).wait_recv()

    @pl.when(core == 0)
    def _():
        core_image.wait_recv()
        text_side(i1, ids_in[4, 1:2, :])

    @pl.when(core == 1)
    def _():
        core_text.wait_recv()
        image_side(t1, ids_in[4, 0:1, :])

    @pl.when(first)
    def _():
        for s in range(5, N_Z):
            pl.semaphore_wait(ready_strip.at[s], 1)
            strip_image(s).start()

    @pl.when(z > 0)
    def _():
        strip_image(0).wait_recv()

    @pl.when(jnp.logical_not(last))
    def _():
        pl.semaphore_wait(ready_wrap, 1)

    @pl.when(z > 0)
    def _():
        pass_image.start()

    @pl.when(first)
    def _():
        own_image.start()
        ids_prev.start()

    for c in range(2, N_CHUNK):
        group_image(c).start()

    @pl.when(jnp.logical_not(last))
    def _():
        strip_text(0).wait_recv()
        pass_text.start()

    for c in range(2, N_CHUNK):
        group_text(c).start()

    whole_text = remote(th, t2, send_sem.at[0], block_recv.at[0], k_next)
    whole_image = remote(ih, i2, send_sem.at[2], block_recv.at[1], k_prev)
    ids_prev.wait_recv()
    whole_image.wait_recv()

    @pl.when(core == 0)
    def _():
        ids_on_image.start()
        on_image.start()

    text_side(i2, ids_in[3, 1:2, :])
    ids_next.wait_recv()
    whole_text.wait_recv()

    @pl.when(core == 1)
    def _():
        ids_on_text.start()
        on_text.start()

    image_side(t2, ids_in[2, 0:1, :])
    ids_on_text.wait_recv()

    @pl.when(core == 0)
    def _():
        on_text.wait_recv()
        image_side(t1, ids_in[5, 0:1, :])

    @pl.when(core == 1)
    def _():
        on_image.wait_recv()
        text_side(i1, ids_in[5, 1:2, :])

    ids_copies[0].wait_recv()
    ids_copies[1].wait_recv()
    for c in range(N_CHUNK):
        here = c * CHUNK
        group_text(c).wait_recv()
        image_side(tg, ids_in[0, 0:1, here:here + CHUNK], here, CHUNK)
        group_image(c).wait_recv()
        text_side(ig, ids_in[1, 1:2, here:here + CHUNK], here, CHUNK)

    def backward(raw, inv_ref, acc, out):
        def step(r, carry):
            rows = pl.ds(pl.multiple_of(r * 32, 32), 32)
            inv = inv_ref[rows, 0:1]
            unit = raw[rows, :] * inv
            grad = acc[rows, :]
            out[rows, :] = inv * (grad - unit * jnp.sum(unit * grad, axis=-1, keepdims=True))
            return carry

        lax.fori_loop(0, ROWS // 32, step, 0)

    backward(im, inv_i, acc_i, image_out)
    backward(tx, inv_t, acc_t, text_out)
    loss_out[...] = loss_acc[...].T[0:1, :]

    for c in range(N_CHUNK):
        group_text(c).wait_send()
        group_image(c).wait_send()
    for copy in ids_copies:
        copy.wait_send()
    ids_next.wait_send()
    ids_prev.wait_send()
    ids_on_text.wait_send()
    core_text.wait_send()
    on_text.wait_send()

    @pl.when(z > 0)
    def _():
        prev_image(0).wait_send()
        prev_image(1).wait_send()

    @pl.when(jnp.logical_not(last))
    def _():
        next_text(0).wait_send()
        next_text(1).wait_send()

    pass_text.wait_send()
    pass_image.wait_send()

    @pl.when(last)
    def _():
        for s in range(N_Z - 1):
            strip_text(s).wait_send()

    @pl.when(first)
    def _():
        for s in range(1, N_Z):
            strip_image(s).wait_send()


def local(images, texts, image_ids, text_ids, log_scale, bias):
    block = pltpu.VMEM((ROWS, D), BF16)
    wide = pltpu.VMEM((ROWS, D), F32)
    lanes = pltpu.VMEM((ROWS, 128), F32)
    dma, plain = pltpu.SemaphoreType.DMA, pltpu.SemaphoreType.REGULAR
    vmem = pl.BlockSpec(memory_space=pltpu.VMEM)
    smem = pl.BlockSpec(memory_space=pltpu.SMEM)
    hbm = pl.BlockSpec(memory_space=pl.ANY)
    row_loss, image_grad, text_grad = pl.pallas_call(
        kernel,
        out_shape=(
            jax.ShapeDtypeStruct((1, ROWS), F32),
            jax.ShapeDtypeStruct((ROWS, D), F32),
            jax.ShapeDtypeStruct((ROWS, D), F32),
        ),
        in_specs=[hbm, hbm, vmem, vmem, smem, smem],
        out_specs=(vmem, vmem, vmem),
        scratch_shapes=[
            wide, wide, block, block, lanes, lanes, wide, wide, lanes, lanes, lanes,
            pltpu.VMEM((8, ROWS), jnp.int32),
            block, block, block, block, block, block,
            pltpu.VMEM((STRIP, D), BF16), pltpu.VMEM((STRIP, D), BF16),
            pltpu.VMEM((6, 8, ROWS), jnp.int32),
            dma((2, N_CHUNK)), dma((8,)), dma((2, N_CHUNK)), dma((2, N_CHUNK)), dma((6,)),
            dma((6,)), dma((6,)), dma((N_Z,)), plain, plain((N_Z,)), plain,
        ],
        compiler_params=pltpu.CompilerParams(
            collective_id=0, has_side_effects=True, vmem_limit_bytes=48 * 1024 * 1024
        ),
    )(images, texts, image_ids.reshape(1, ROWS), text_ids.reshape(1, ROWS), log_scale, bias)
    return row_loss.reshape(ROWS), image_grad, text_grad


def solution(mesh):
    rows, wide = P(("group", "blk")), P(("group", "blk"), None)
    return jax.shard_map(
        local,
        mesh=mesh,
        in_specs=(wide, wide, rows, rows, P(), P()),
        out_specs=(rows, wide, wide),
        check_vma=False,
    )
```

```python
import functools

import jax
import jax.numpy as jnp
from jax import lax
from jax.experimental import pallas as pl
from jax.experimental.pallas import tpu as pltpu
from jax.sharding import PartitionSpec as P

MESH = pl.DeviceIdType.MESH
ROWS = 256
D = 1152
N_Z = 8
N_YHI = 4
N_GROUP = 8
STRIP = ROWS // N_Z
CHUNK = 64
N_CHUNK = ROWS // CHUNK
N_FIRST_TEXT = 1
N_FIRST_IMAGE = 3
TILE = 384
F32 = jnp.float32
BF16 = jnp.bfloat16


def rows_of(ref, start, count):
    return ref.at[pl.ds(start, count)]


def kernel(
    images, texts, image_ids, text_ids, log_scale, bias,
    im, tx, inv_i, inv_t, acc_i, acc_t, loss_acc,
    ih, th, col_i, col_t, id_rows, ids,
    t1, t2, tg, i1, i2, ig, relay_t, relay_i, ids_in,
    load_sem, id_sem, send_sem, chunk_send, chunk_recv, block_recv, ids_send, ids_recv, strip_send, ready_next, ready_strip, ready_wrap,
):
    g = lax.axis_index("group")
    k = lax.axis_index("blk")
    core = lax.rem(k, 2)
    z = lax.rem(k // 2, N_Z)
    yhi = k // (2 * N_Z)
    first, last = z == 0, z == N_Z - 1

    def at(yh, zz, cc):
        return (g, (lax.rem(yh + N_YHI, N_YHI) * N_Z + zz) * 2 + cc)

    g_next = (lax.rem(g + 1, N_GROUP), k)
    g_prev = (lax.rem(g + N_GROUP - 1, N_GROUP), k)
    partner = (g, k + 1 - 2 * core)
    wrap_next = at(yhi + 1, 0, core)
    wrap_prev = at(yhi - 1, N_Z - 1, core)
    k_next = (g, lax.rem(k + 2, 2 * N_Z * N_YHI))
    k_prev = (g, lax.rem(k + 2 * N_Z * N_YHI - 2, 2 * N_Z * N_YHI))

    barrier = pltpu.get_barrier_semaphore()

    def tell(device):
        pl.semaphore_signal(barrier, inc=1, device_id=device, device_id_type=MESH)

    tell(g_next)
    tell(g_prev)
    tell(partner)

    loads = []
    id_loads = [
        pltpu.make_async_copy(src, id_rows.at[a], id_sem.at[a])
        for a, src in enumerate((text_ids, image_ids))
    ]
    for c in range(N_CHUNK):
        for a, (src, dst) in enumerate(((texts, tx), (images, im))):
            rows = pl.ds(c * CHUNK, CHUNK)
            copy = pltpu.make_async_copy(src.at[rows], dst.at[rows], load_sem.at[a, c])
            copy.start()
            loads.append(copy)
        if c == 0:
            for copy in id_loads:
                copy.start()

    @pl.when(jnp.logical_not(last))
    def _():
        tell(k_next)
        tell(at(yhi, N_Z - 1, core))
        tell(wrap_prev)

    @pl.when(last)
    def _():
        tell(at(yhi + 1, N_Z - 1, core))

    @pl.when(first)
    def _():
        for s in range(N_Z):
            tell(at(yhi - 1, s, core))
        for s in range(1, N_Z):
            tell(at(yhi, s, core))

    scale = jnp.exp(jnp.full((1, 1), log_scale[0], F32))
    offset = bias[0]

    def remote(src, dst, send, recv, device):
        return pltpu.make_async_remote_copy(
            src_ref=src, dst_ref=dst, send_sem=send, recv_sem=recv,
            device_id=device, device_id_type=MESH,
        )

    def group_text(c):
        return remote(rows_of(th, c * CHUNK, CHUNK), rows_of(tg, c * CHUNK, CHUNK),
                      chunk_send.at[0, c], chunk_recv.at[0, c], g_next)

    def group_image(c):
        return remote(rows_of(ih, c * CHUNK, CHUNK), rows_of(ig, c * CHUNK, CHUNK),
                      chunk_send.at[1, c], chunk_recv.at[1, c], g_prev)

    half = ROWS // 2

    def next_text(part):
        return remote(rows_of(th, part * half, half), rows_of(t2, part * half, half),
                      send_sem.at[part], block_recv.at[0], k_next)

    def prev_image(part):
        return remote(rows_of(ih, part * half, half), rows_of(i2, part * half, half),
                      send_sem.at[2 + part], block_recv.at[1], k_prev)

    def strip_text(s):
        return remote(rows_of(th, (s + 1) * STRIP, STRIP), relay_t, strip_send.at[s], block_recv.at[2], at(yhi, s, core))

    def strip_image(s):
        return remote(rows_of(ih, s * STRIP, STRIP), relay_i, strip_send.at[s], block_recv.at[3], at(yhi, s, core))

    mine = pl.multiple_of(z * STRIP, STRIP)
    after = pl.multiple_of(lax.rem(z + 1, N_Z) * STRIP, STRIP)
    pass_text = remote(relay_t, rows_of(t2, after, STRIP), send_sem.at[4], block_recv.at[0], wrap_next)
    pass_image = remote(relay_i, rows_of(i2, mine, STRIP), send_sem.at[5], block_recv.at[1], wrap_prev)
    own_text = remote(rows_of(th, 0, STRIP), rows_of(t2, 0, STRIP), send_sem.at[4], block_recv.at[0], wrap_next)
    own_image = remote(rows_of(ih, 0, STRIP), rows_of(i2, 0, STRIP), send_sem.at[5], block_recv.at[1], wrap_prev)

    core_text = remote(th, t1, send_sem.at[6], block_recv.at[4], partner)
    core_image = remote(ih, i1, send_sem.at[6], block_recv.at[5], partner)
    on_text = remote(t2, t1, send_sem.at[7], block_recv.at[4], partner)
    on_image = remote(i2, i1, send_sem.at[7], block_recv.at[5], partner)

    def send_ids(slot, device, src=ids):
        return remote(src, ids_in.at[slot], ids_send.at[slot], ids_recv.at[slot], device)

    ids_next, ids_prev = send_ids(2, k_next), send_ids(3, k_prev)
    ids_copies = [send_ids(0, g_next), send_ids(1, g_prev), send_ids(4, partner)]
    ids_on_text = send_ids(5, partner, ids_in.at[2])
    ids_on_image = send_ids(5, partner, ids_in.at[3])

    def normalize(c, raw, half_ref, inv_ref):
        rows = pl.ds(c * CHUNK, CHUNK)
        values = raw[rows, :]
        inv = lax.rsqrt(jnp.sum(values * values, axis=-1, keepdims=True) + 1e-06)
        half_ref[rows, :] = (values * inv).astype(BF16)
        inv_ref[rows, :] = jnp.broadcast_to(inv, (CHUNK, 128))

    for c in range(N_CHUNK):
        loads[2 * c].wait()
        normalize(c, tx, th, inv_t)
        if c == 0:
            pl.semaphore_wait(
                barrier, 4 + 2 * (z > 0).astype(jnp.int32) + 15 * last.astype(jnp.int32)
            )

        @pl.when(last)
        def _():
            if c == 0:
                own_text.start()
            for r in range(c * CHUNK // STRIP, (c + 1) * CHUNK // STRIP):
                if r > 0:
                    strip_text(r - 1).start()

        if c < N_FIRST_TEXT:
            group_text(c).start()

        if c == 0:
            @pl.when(z > 0)
            def _():
                pl.semaphore_signal(ready_next, inc=1, device_id=k_prev, device_id_type=MESH)
                pl.semaphore_signal(ready_strip.at[z], inc=1, device_id=at(yhi, 0, core), device_id_type=MESH)

            @pl.when(last)
            def _():
                for s in range(N_Z - 1):
                    pl.semaphore_signal(ready_wrap, inc=1, device_id=at(yhi + 1, s, core), device_id_type=MESH)

        loads[2 * c + 1].wait()
        normalize(c, im, ih, inv_i)
        if c < N_FIRST_IMAGE:
            group_image(c).start()

    for copy in id_loads:
        copy.wait()
    ids[...] = jnp.concatenate(
        [id_rows[0], id_rows[1], jnp.zeros((6, ROWS), jnp.int32)], axis=0
    )
    col_t[...] = jnp.broadcast_to(id_rows[0].astype(F32), (128, ROWS)).T
    col_i[...] = jnp.broadcast_to(id_rows[1].astype(F32), (128, ROWS)).T
    for copy in ids_copies:
        copy.start()

    @pl.when(core == 0)
    def _():
        core_text.start()

    @pl.when(core == 1)
    def _():
        core_image.start()

    @pl.when(z > 0)
    def _():
        ids_prev.start()
        prev_image(0).start()
        prev_image(1).start()

    @pl.when(jnp.logical_not(last))
    def _():
        pl.semaphore_wait(ready_next, 1)
        ids_next.start()
        next_text(0).start()

    @pl.when(last)
    def _():
        ids_next.start()

    @pl.when(jnp.logical_not(last) & (z > 0))
    def _():
        next_text(1).start()

    def side(own_half, own_col, other, start, count, other_ids, acc, loss, fresh=False):
        block = other[pl.ds(start, count), :]
        dots = lax.dot_general(
            own_half[...], block, (((1,), (1,)), ((), ())), preferred_element_type=F32
        )
        logit = scale * dots + offset
        same = own_col[:, 0:1] == other_ids.astype(F32)
        u = jnp.where(same, -logit, logit)
        e = jnp.exp(-jnp.abs(u))
        coeff = jnp.where(same, -scale, scale) * (jnp.where(u >= 0, 1.0, e) / (1.0 + e))
        coeff = coeff.astype(BF16)
        if loss is not None:
            terms = jnp.maximum(u, 0.0) + jnp.log1p(e)
            terms = jnp.sum(terms, axis=1, keepdims=True)
            terms = jnp.broadcast_to(terms, (ROWS, 128))
            loss[...] = terms if fresh else loss[...] + terms

        for t in range(0, D, TILE):
            cols = pl.ds(t, TILE)
            term = jnp.dot(coeff, other[pl.ds(start, count), cols], preferred_element_type=F32)
            acc[:, cols] = term if fresh else acc[:, cols] + term

    def image_side(block, text_row, start=0, count=ROWS, fresh=False):
        side(ih, col_i, block, start, count, text_row, acc_i, loss_acc, fresh)

    def text_side(block, image_row, start=0, count=ROWS, fresh=False):
        side(th, col_t, block, start, count, image_row, acc_t, None, fresh)

    image_side(th, ids[0:1, :], fresh=True)

    @pl.when(first)
    def _():
        for s in range(1, 5):
            pl.semaphore_wait(ready_strip.at[s], 1)
            strip_image(s).start()
        next_text(1).start()

    text_side(ih, ids[1:2, :], fresh=True)

    send_ids(4, partner).wait_recv()

    @pl.when(core == 0)
    def _():
        core_image.wait_recv()
        text_side(i1, ids_in[4, 1:2, :])

    @pl.when(core == 1)
    def _():
        core_text.wait_recv()
        image_side(t1, ids_in[4, 0:1, :])

    @pl.when(first)
    def _():
        for s in range(5, N_Z):
            pl.semaphore_wait(ready_strip.at[s], 1)
            strip_image(s).start()

    @pl.when(jnp.logical_not(last))
    def _():
        strip_text(0).wait_recv()
        pass_text.start()

    for c in range(N_FIRST_TEXT, N_CHUNK):
        group_text(c).start()

    @pl.when(z > 0)
    def _():
        strip_image(0).wait_recv()

    @pl.when(jnp.logical_not(last))
    def _():
        pl.semaphore_wait(ready_wrap, 1)

    @pl.when(z > 0)
    def _():
        pass_image.start()

    @pl.when(first)
    def _():
        own_image.start()
        ids_prev.start()

    for c in range(N_FIRST_IMAGE, N_CHUNK):
        group_image(c).start()

    whole_text = remote(th, t2, send_sem.at[0], block_recv.at[0], k_next)
    whole_image = remote(ih, i2, send_sem.at[2], block_recv.at[1], k_prev)

    def meet_image():
        ids_prev.wait_recv()
        whole_image.wait_recv()

        @pl.when(core == 0)
        def _():
            ids_on_image.start()
            on_image.start()

        text_side(i2, ids_in[3, 1:2, :])

    def meet_text():
        ids_next.wait_recv()
        whole_text.wait_recv()

        @pl.when(core == 1)
        def _():
            ids_on_text.start()
            on_text.start()

        image_side(t2, ids_in[2, 0:1, :])

    def meet_passed_text():
        ids_on_text.wait_recv()
        on_text.wait_recv()
        image_side(t1, ids_in[5, 0:1, :])

    def meet_passed_image():
        ids_on_image.wait_recv()
        on_image.wait_recv()
        text_side(i1, ids_in[5, 1:2, :])

    pl.when(jnp.logical_not(last))(meet_image)
    pl.when(jnp.logical_not(first))(meet_text)
    pl.when(jnp.logical_not(last) & (core == 1))(meet_passed_image)
    pl.when(jnp.logical_not(first) & (core == 0))(meet_passed_text)

    ids_copies[0].wait_recv()
    ids_copies[1].wait_recv()

    def meet_group(begin, stop):
        here, count = begin * CHUNK, (stop - begin) * CHUNK
        for c in range(begin, stop):
            group_text(c).wait_recv()
        image_side(tg, ids_in[0, 0:1, here:here + count], here, count)
        for c in range(begin, stop):
            group_image(c).wait_recv()
        text_side(ig, ids_in[1, 1:2, here:here + count], here, count)

    meet_group(0, N_CHUNK - 1)
    pl.when(last)(meet_image)
    pl.when(first)(meet_text)
    pl.when(last & (core == 1))(meet_passed_image)
    pl.when(first & (core == 0))(meet_passed_text)
    meet_group(N_CHUNK - 1, N_CHUNK)

    for c in range(N_CHUNK):
        group_text(c).wait_send()
        group_image(c).wait_send()
    for copy in ids_copies:
        copy.wait_send()
    ids_next.wait_send()
    ids_prev.wait_send()
    ids_on_text.wait_send()
    core_text.wait_send()
    on_text.wait_send()

    @pl.when(z > 0)
    def _():
        prev_image(0).wait_send()
        prev_image(1).wait_send()

    @pl.when(jnp.logical_not(last))
    def _():
        next_text(0).wait_send()
        next_text(1).wait_send()

    pass_text.wait_send()
    pass_image.wait_send()

    @pl.when(last)
    def _():
        for s in range(N_Z - 1):
            strip_text(s).wait_send()

    @pl.when(first)
    def _():
        for s in range(1, N_Z):
            strip_image(s).wait_send()


def finish(im, tx, inv_i, inv_t, acc_i, acc_t, loss_acc, loss_out, image_out, text_out, row, image_buf, text_buf, sems):
    row[...] = loss_acc[...].T[0:1, :]
    loss_copy = pltpu.make_async_copy(row, loss_out, sems.at[2, 0])
    loss_copy.start()
    copies = [loss_copy]
    for a, (raw, inv_ref, acc, buf, out) in enumerate(
        ((im, inv_i, acc_i, image_buf, image_out), (tx, inv_t, acc_t, text_buf, text_out))
    ):
        for c in range(N_CHUNK):
            rows = pl.ds(c * CHUNK, CHUNK)
            inv = inv_ref[rows, 0:1]
            unit = raw[rows, :] * inv
            grad = acc[rows, :]
            buf[rows, :] = inv * (grad - unit * jnp.sum(unit * grad, axis=-1, keepdims=True))
            copy = pltpu.make_async_copy(buf.at[rows], out.at[rows], sems.at[a, c])
            copy.start()
            copies.append(copy)
    for copy in copies:
        copy.wait()


def local(images, texts, image_ids, text_ids, log_scale, bias):
    block = pltpu.VMEM((ROWS, D), BF16)
    wide = pltpu.VMEM((ROWS, D), F32)
    lanes = pltpu.VMEM((ROWS, 128), F32)
    wide_out = jax.ShapeDtypeStruct((ROWS, D), F32)
    lanes_out = jax.ShapeDtypeStruct((ROWS, 128), F32)
    dma, plain = pltpu.SemaphoreType.DMA, pltpu.SemaphoreType.REGULAR
    vmem = pl.BlockSpec(memory_space=pltpu.VMEM)
    smem = pl.BlockSpec(memory_space=pltpu.SMEM)
    hbm = pl.BlockSpec(memory_space=pltpu.HBM)
    given = (images, texts, image_ids.reshape(1, ROWS), text_ids.reshape(1, ROWS))
    in_hbm = [pltpu.with_memory_space_constraint(a, pltpu.HBM) for a in given]
    parts = pl.pallas_call(
        kernel,
        out_shape=(wide_out, wide_out, lanes_out, lanes_out, wide_out, wide_out, lanes_out),
        in_specs=[hbm, hbm, hbm, hbm, smem, smem],
        out_specs=(vmem,) * 7,
        scratch_shapes=[
            block, block, lanes, lanes, pltpu.VMEM((2, 1, ROWS), jnp.int32),
            pltpu.VMEM((8, ROWS), jnp.int32),
            block, block, block, block, block, block,
            pltpu.VMEM((STRIP, D), BF16), pltpu.VMEM((STRIP, D), BF16),
            pltpu.VMEM((6, 8, ROWS), jnp.int32),
            dma((2, N_CHUNK)), dma((2,)), dma((8,)), dma((2, N_CHUNK)), dma((2, N_CHUNK)), dma((6,)),
            dma((6,)), dma((6,)), dma((N_Z,)), plain, plain((N_Z,)), plain,
        ],
        compiler_params=pltpu.CompilerParams(
            collective_id=0, has_side_effects=True, vmem_limit_bytes=32 * 1024 * 1024
        ),
    )(*in_hbm, log_scale, bias)
    row_loss, image_grad, text_grad = pl.pallas_call(
        finish,
        out_shape=(jax.ShapeDtypeStruct((1, ROWS), F32), wide_out, wide_out),
        in_specs=[vmem] * 7,
        out_specs=(hbm,) * 3,
        scratch_shapes=[pltpu.VMEM((1, ROWS), F32), wide, wide, dma((3, N_CHUNK))],
        compiler_params=pltpu.CompilerParams(vmem_limit_bytes=16 * 1024 * 1024),
    )(*parts)
    return row_loss.reshape(ROWS), image_grad, text_grad


def solution(mesh):
    rows, wide = P(("group", "blk")), P(("group", "blk"), None)
    return jax.shard_map(
        local,
        mesh=mesh,
        in_specs=(wide, wide, rows, rows, P(), P()),
        out_specs=(rows, wide, wide),
        check_vma=False,
    )
```

```python
import functools

import jax
import jax.numpy as jnp
from jax import lax
from jax.experimental import pallas as pl
from jax.experimental.pallas import tpu as pltpu
from jax.sharding import PartitionSpec as P

MESH = pl.DeviceIdType.MESH
ROWS = 256
D = 1152
N_Z = 8
N_YHI = 4
N_GROUP = 8
STRIP = ROWS // N_Z
CHUNK = 64
N_CHUNK = ROWS // CHUNK
N_EARLY = 3
TILE = 384
F32 = jnp.float32
BF16 = jnp.bfloat16


def rows_of(ref, start, count):
    return ref.at[pl.ds(start, count)]


def backward(raw, inv, grad):
    unit = raw * inv
    return inv * (grad - unit * jnp.sum(unit * grad, axis=-1, keepdims=True))


def kernel(
    images, texts, image_ids, text_ids, log_scale, bias,
    tx, inv_t, image_grad, acc_t, loss_acc,
    im, inv_i, acc_i, ih, th, col_i, col_t, id_rows, ids,
    t1, t2, tg, i1, i2, ig, relay_t, relay_i, ids_in,
    load_sem, id_sem, send_sem, chunk_send, chunk_recv, block_recv, two_recv, pass_send, pass_recv, next_send, prev_send, ids_send, ids_recv, strip_send, ready_next, ready_strip, ready_wrap,
):
    g = lax.axis_index("group")
    k = lax.axis_index("blk")
    core = lax.rem(k, 2)
    z = lax.rem(k // 2, N_Z)
    yhi = k // (2 * N_Z)
    first, last = z == 0, z == N_Z - 1

    even = 2 * (1 - lax.rem(g, 2))
    relay_g = lax.rem(g + N_GROUP - even, N_GROUP)
    from_g = lax.rem(g + even, N_GROUP)

    def at(yh, zz, cc, gg=g):
        return (gg, (lax.rem(yh + N_YHI, N_YHI) * N_Z + zz) * 2 + cc)

    g_next = (lax.rem(g + 1, N_GROUP), k)
    g_prev = (lax.rem(g + N_GROUP - 1, N_GROUP), k)
    partner = (g, k + 1 - 2 * core)
    wrap_next = at(yhi + 1, 0, core)
    wrap_prev = at(yhi - 1, N_Z - 1, core)
    k_next = (g, lax.rem(k + 2, 2 * N_Z * N_YHI))
    k_prev = (g, lax.rem(k + 2 * N_Z * N_YHI - 2, 2 * N_Z * N_YHI))

    barrier = pltpu.get_barrier_semaphore()

    def tell(device):
        pl.semaphore_signal(barrier, inc=1, device_id=device, device_id_type=MESH)

    tell(g_next)
    tell(g_prev)
    tell(partner)

    loads = []
    id_loads = [
        pltpu.make_async_copy(src, id_rows.at[a], id_sem.at[a])
        for a, src in enumerate((text_ids, image_ids))
    ]
    for a, (src, dst) in enumerate(((texts, tx), (images, im))):
        for c in range(N_CHUNK):
            rows = pl.ds(c * CHUNK, CHUNK)
            copy = pltpu.make_async_copy(src.at[rows], dst.at[rows], load_sem.at[a, c])
            loads.append(copy)
    for copy in loads[:N_CHUNK] + id_loads:
        copy.start()

    @pl.when(jnp.logical_not(last))
    def _():
        tell(k_next)
        tell(at(yhi, N_Z - 1, core, from_g))
        tell(wrap_prev)

    @pl.when(last)
    def _():
        tell(at(yhi + 1, N_Z - 1, core))

    @pl.when(first)
    def _():
        tell(wrap_prev)
        for s in range(N_Z - 1):
            tell(at(yhi - 1, s, core, relay_g))
        for s in range(1, N_Z):
            tell(at(yhi, s, core))

    scale = jnp.exp(jnp.full((1, 1), log_scale[0], F32))
    offset = bias[0]

    def remote(src, dst, send, recv, device):
        return pltpu.make_async_remote_copy(
            src_ref=src, dst_ref=dst, send_sem=send, recv_sem=recv,
            device_id=device, device_id_type=MESH,
        )

    def group_text(c):
        return remote(rows_of(th, c * CHUNK, CHUNK), rows_of(tg, c * CHUNK, CHUNK),
                      chunk_send.at[0, c], chunk_recv.at[0, c], g_next)

    def group_image(c):
        return remote(rows_of(ih, c * CHUNK, CHUNK), rows_of(ig, c * CHUNK, CHUNK),
                      chunk_send.at[1, c], chunk_recv.at[1, c], g_prev)

    def next_text(part):
        return remote(rows_of(th, part * CHUNK, CHUNK), rows_of(t2, part * CHUNK, CHUNK),
                      next_send.at[part], two_recv.at[0, part], k_next)

    def prev_image(part):
        return remote(rows_of(ih, part * CHUNK, CHUNK), rows_of(i2, part * CHUNK, CHUNK),
                      prev_send.at[part], two_recv.at[1, part], k_prev)

    def strip_text(s):
        return remote(rows_of(th, (s + 1) * STRIP, STRIP), relay_t, strip_send.at[s], block_recv.at[2], at(yhi, s, core, relay_g))

    def strip_image(s):
        return remote(rows_of(ih, s * STRIP, STRIP), relay_i, strip_send.at[s], block_recv.at[3], at(yhi, s, core))

    mine = pl.multiple_of(z * STRIP, STRIP)
    after = pl.multiple_of(lax.rem(z + 1, N_Z) * STRIP, STRIP)
    pass_text = remote(relay_t, rows_of(t2, after, STRIP), send_sem.at[4], two_recv.at[0, after // CHUNK], at(yhi + 1, 0, core, from_g))
    pass_image = remote(relay_i, rows_of(i2, mine, STRIP), send_sem.at[5], two_recv.at[1, mine // CHUNK], wrap_prev)
    own_text = remote(rows_of(th, 0, STRIP), rows_of(t2, 0, STRIP), send_sem.at[4], two_recv.at[0, 0], wrap_next)
    own_image = remote(rows_of(ih, 0, STRIP), rows_of(i2, 0, STRIP), send_sem.at[5], two_recv.at[1, 0], wrap_prev)

    core_text = remote(th, t1, send_sem.at[6], block_recv.at[4], partner)
    core_image = remote(ih, i1, send_sem.at[6], block_recv.at[5], partner)

    def on_text(part):
        return remote(rows_of(t2, part * CHUNK, CHUNK), rows_of(t1, part * CHUNK, CHUNK),
                      pass_send.at[part], pass_recv.at[part], partner)

    def on_image(part):
        return remote(rows_of(i2, part * CHUNK, CHUNK), rows_of(i1, part * CHUNK, CHUNK),
                      pass_send.at[part], pass_recv.at[part], partner)

    def send_ids(slot, device, src=ids):
        return remote(src, ids_in.at[slot], ids_send.at[slot], ids_recv.at[slot], device)

    ids_next, ids_prev = send_ids(2, k_next), send_ids(3, k_prev)
    ids_copies = [send_ids(0, g_next), send_ids(1, g_prev), send_ids(4, partner)]
    ids_on_text = send_ids(5, partner, ids_in.at[2])
    ids_on_image = send_ids(5, partner, ids_in.at[3])

    def normalize(c, raw, half_ref, inv_ref):
        rows = pl.ds(c * CHUNK, CHUNK)
        values = raw[rows, :]
        inv = lax.rsqrt(jnp.sum(values * values, axis=-1, keepdims=True) + 1e-06)
        half_ref[rows, :] = (values * inv).astype(BF16)
        inv_ref[rows, :] = jnp.broadcast_to(inv, (CHUNK, 128))

    for c in range(N_CHUNK):
        loads[c].wait()
        if c == 0:
            for copy in loads[N_CHUNK:]:
                copy.start()
        normalize(c, tx, th, inv_t)
        if c == 0:
            pl.semaphore_wait(
                barrier, 4 + 2 * (z > 0).astype(jnp.int32) + 15 * last.astype(jnp.int32)
            )

        @pl.when(last)
        def _():
            if c == 0:
                own_text.start()
            for r in range(c * CHUNK // STRIP, (c + 1) * CHUNK // STRIP):
                if r > 0:
                    strip_text(r - 1).start()

        group_text(c).start()
        if c == 0:
            @pl.when(z > 0)
            def _():
                pl.semaphore_signal(ready_next, inc=1, device_id=k_prev, device_id_type=MESH)
                pl.semaphore_signal(ready_strip.at[z], inc=1, device_id=at(yhi, 0, core), device_id_type=MESH)

            @pl.when(last)
            def _():
                for s in range(N_Z - 1):
                    pl.semaphore_signal(ready_wrap, inc=1, device_id=at(yhi + 1, s, core), device_id_type=MESH)

    @pl.when(core == 0)
    def _():
        core_text.start()

    @pl.when(jnp.logical_not(last))
    def _():
        pl.semaphore_wait(ready_next, 1)
        next_text(0).start()
        next_text(1).start()

    @pl.when(jnp.logical_not(last) & (z > 0))
    def _():
        next_text(2).start()
        next_text(3).start()

    for c in range(N_CHUNK):
        loads[N_CHUNK + c].wait()
        normalize(c, im, ih, inv_i)
        pl.when(z > 0)(prev_image(c).start)

    @pl.when(core == 1)
    def _():
        core_image.start()

    for copy in id_loads:
        copy.wait()
    ids[...] = jnp.concatenate(
        [id_rows[0], id_rows[1], jnp.zeros((6, ROWS), jnp.int32)], axis=0
    )
    col_t[...] = jnp.broadcast_to(id_rows[0].astype(F32), (128, ROWS)).T
    col_i[...] = jnp.broadcast_to(id_rows[1].astype(F32), (128, ROWS)).T
    for copy in ids_copies:
        copy.start()

    ids_next.start()
    pl.when(z > 0)(ids_prev.start)

    def side(own_half, own_col, other, start, count, other_ids, acc, loss, fresh=False):
        block = other[pl.ds(start, count), :]
        dots = lax.dot_general(
            own_half[...], block, (((1,), (1,)), ((), ())), preferred_element_type=F32
        )
        logit = scale * dots + offset
        same = own_col[:, 0:1] == other_ids.astype(F32)
        u = jnp.where(same, -logit, logit)
        e = jnp.exp(-jnp.abs(u))
        coeff = jnp.where(same, -scale, scale) * (jnp.where(u >= 0, 1.0, e) / (1.0 + e))
        coeff = coeff.astype(BF16)
        if loss is not None:
            terms = jnp.maximum(u, 0.0) + jnp.log1p(e)
            terms = jnp.sum(terms, axis=1, keepdims=True)
            terms = jnp.broadcast_to(terms, (ROWS, 128))
            loss[...] = terms if fresh else loss[...] + terms

        for t in range(0, D, TILE):
            cols = pl.ds(t, TILE)
            term = jnp.dot(coeff, other[pl.ds(start, count), cols], preferred_element_type=F32)
            acc[:, cols] = term if fresh else acc[:, cols] + term

    def image_side(block, text_row, start=0, count=ROWS, fresh=False):
        side(ih, col_i, block, start, count, text_row, acc_i, loss_acc, fresh)

    def text_side(block, image_row, start=0, count=ROWS, fresh=False):
        side(th, col_t, block, start, count, image_row, acc_t, None, fresh)

    image_side(th, ids[0:1, :], fresh=True)

    @pl.when(first)
    def _():
        for s in range(1, 5):
            pl.semaphore_wait(ready_strip.at[s], 1)
            strip_image(s).start()
        next_text(2).start()
        next_text(3).start()

    text_side(ih, ids[1:2, :], fresh=True)

    send_ids(4, partner).wait_recv()

    @pl.when(core == 0)
    def _():
        core_image.wait_recv()
        text_side(i1, ids_in[4, 1:2, :])

    @pl.when(core == 1)
    def _():
        core_text.wait_recv()
        image_side(t1, ids_in[4, 0:1, :])

    @pl.when(first)
    def _():
        for s in range(5, N_Z):
            pl.semaphore_wait(ready_strip.at[s], 1)
            strip_image(s).start()

    @pl.when((z >= N_EARLY) & jnp.logical_not(last))
    def _():
        strip_text(0).wait_recv()
        pass_text.start()

    for c in range(N_CHUNK - 1):
        group_text(c).wait_send()
    group_image(0).start()

    @pl.when(z < N_EARLY)
    def _():
        strip_text(0).wait_recv()
        pass_text.start()

    group_image(1).start()

    def relay_image():
        @pl.when(z > 0)
        def _():
            strip_image(0).wait_recv()

        @pl.when(jnp.logical_not(last))
        def _():
            pl.semaphore_wait(ready_wrap, 1)

        pl.when(z > 0)(pass_image.start)

        @pl.when(first)
        def _():
            own_image.start()
            ids_prev.start()

        for c in range(2, N_CHUNK):
            group_image(c).start()

    def meet_image():
        ids_prev.wait_recv()
        pl.when(core == 0)(ids_on_image.start)
        for part in range(N_CHUNK):
            prev_image(part).wait_recv()
            pl.when(core == 0)(on_image(part).start)
        text_side(i2, ids_in[3, 1:2, :])

    def meet_text():
        ids_next.wait_recv()
        pl.when(core == 1)(ids_on_text.start)
        for part in range(N_CHUNK):
            next_text(part).wait_recv()
            pl.when(core == 1)(on_text(part).start)
        image_side(t2, ids_in[2, 0:1, :])

    def meet_passed_text():
        ids_on_text.wait_recv()
        for part in range(N_CHUNK):
            on_text(part).wait_recv()
        image_side(t1, ids_in[5, 0:1, :])

    def meet_passed_image():
        ids_on_image.wait_recv()
        for part in range(N_CHUNK):
            on_image(part).wait_recv()
        text_side(i1, ids_in[5, 1:2, :])

    pl.when((z < 2) | (z >= 6))(relay_image)
    pl.when(jnp.logical_not(first))(meet_text)
    pl.when((z >= 2) & (z < 6))(relay_image)
    pl.when(jnp.logical_not(last))(meet_image)
    pl.when(jnp.logical_not(last) & (core == 1))(meet_passed_image)
    pl.when(jnp.logical_not(first) & (core == 0))(meet_passed_text)

    ids_copies[0].wait_recv()
    ids_copies[1].wait_recv()
    for c in range(N_CHUNK):
        group_text(c).wait_recv()
    image_side(tg, ids_in[0, 0:1, :])

    def meet_group_image(begin, stop):
        here, count = begin * CHUNK, (stop - begin) * CHUNK
        for c in range(begin, stop):
            group_image(c).wait_recv()
        text_side(ig, ids_in[1, 1:2, here:here + count], here, count)

    def image_backward():
        for c in range(N_CHUNK):
            rows = pl.ds(c * CHUNK, CHUNK)
            image_grad[rows, :] = backward(im[rows, :], inv_i[rows, 0:1], acc_i[rows, :])

    pl.when(jnp.logical_not(first))(image_backward)
    pl.when(last & (core == 0))(meet_image)
    meet_group_image(0, N_CHUNK - 1)
    pl.when(first & (core == 1))(meet_text)
    pl.when(first & (core == 0))(meet_passed_text)
    pl.when(last & (core == 1))(meet_image)
    pl.when(last & (core == 1))(meet_passed_image)
    meet_group_image(N_CHUNK - 1, N_CHUNK)
    pl.when(first & (core == 0))(meet_text)
    pl.when(first)(image_backward)

    group_text(N_CHUNK - 1).wait_send()
    for c in range(N_CHUNK):
        group_image(c).wait_send()
    for copy in ids_copies:
        copy.wait_send()
    ids_next.wait_send()
    ids_prev.wait_send()
    ids_on_text.wait_send()
    core_text.wait_send()
    for part in range(N_CHUNK):
        on_text(part).wait_send()

    @pl.when(z > 0)
    def _():
        for part in range(N_CHUNK):
            prev_image(part).wait_send()

    @pl.when(jnp.logical_not(last))
    def _():
        for part in range(N_CHUNK):
            next_text(part).wait_send()

    pass_text.wait_send()
    pass_image.wait_send()

    @pl.when(last)
    def _():
        for s in range(N_Z - 1):
            strip_text(s).wait_send()

    @pl.when(first)
    def _():
        for s in range(1, N_Z):
            strip_image(s).wait_send()


def finish(tx, inv_t, image_grad, acc_t, loss_acc, loss_out, image_out, text_out, row, buf, sems):
    image_copy = pltpu.make_async_copy(image_grad, image_out, sems.at[N_CHUNK])
    image_copy.start()
    copies = [image_copy]
    for c in range(N_CHUNK):
        rows = pl.ds(c * CHUNK, CHUNK)
        buf[rows, :] = backward(tx[rows, :], inv_t[rows, 0:1], acc_t[rows, :])
        copy = pltpu.make_async_copy(buf.at[rows], text_out.at[rows], sems.at[c])
        copy.start()
        copies.append(copy)
    row[...] = loss_acc[...].T[0:1, :]
    loss_copy = pltpu.make_async_copy(row, loss_out, sems.at[N_CHUNK + 1])
    loss_copy.start()
    for copy in copies + [loss_copy]:
        copy.wait()


def local(images, texts, image_ids, text_ids, log_scale, bias):
    block = pltpu.VMEM((ROWS, D), BF16)
    wide = pltpu.VMEM((ROWS, D), F32)
    lanes = pltpu.VMEM((ROWS, 128), F32)
    wide_out = jax.ShapeDtypeStruct((ROWS, D), F32)
    lanes_out = jax.ShapeDtypeStruct((ROWS, 128), F32)
    dma, plain = pltpu.SemaphoreType.DMA, pltpu.SemaphoreType.REGULAR
    vmem = pl.BlockSpec(memory_space=pltpu.VMEM)
    smem = pl.BlockSpec(memory_space=pltpu.SMEM)
    hbm = pl.BlockSpec(memory_space=pltpu.HBM)
    given = (images, texts, image_ids.reshape(1, ROWS), text_ids.reshape(1, ROWS))
    in_hbm = [pltpu.with_memory_space_constraint(a, pltpu.HBM) for a in given]
    parts = pl.pallas_call(
        kernel,
        out_shape=(wide_out, lanes_out, wide_out, wide_out, lanes_out),
        in_specs=[hbm, hbm, hbm, hbm, smem, smem],
        out_specs=(vmem,) * 5,
        scratch_shapes=[
            wide, lanes, wide, block, block, lanes, lanes, pltpu.VMEM((2, 1, ROWS), jnp.int32),
            pltpu.VMEM((8, ROWS), jnp.int32),
            block, block, block, block, block, block,
            pltpu.VMEM((STRIP, D), BF16), pltpu.VMEM((STRIP, D), BF16),
            pltpu.VMEM((6, 8, ROWS), jnp.int32),
            dma((2, N_CHUNK)), dma((2,)), dma((8,)), dma((2, N_CHUNK)), dma((2, N_CHUNK)), dma((6,)),
            dma((2, N_CHUNK)), dma((N_CHUNK,)), dma((N_CHUNK,)), dma((N_CHUNK,)), dma((N_CHUNK,)), dma((6,)), dma((6,)), dma((N_Z,)), plain, plain((N_Z,)), plain,
        ],
        compiler_params=pltpu.CompilerParams(
            collective_id=0, has_side_effects=True, vmem_limit_bytes=32 * 1024 * 1024
        ),
    )(*in_hbm, log_scale, bias)
    row_loss, image_grad, text_grad = pl.pallas_call(
        finish,
        out_shape=(jax.ShapeDtypeStruct((1, ROWS), F32), wide_out, wide_out),
        in_specs=[vmem] * 5,
        out_specs=(hbm,) * 3,
        scratch_shapes=[pltpu.VMEM((1, ROWS), F32), wide, dma((N_CHUNK + 2,))],
        compiler_params=pltpu.CompilerParams(vmem_limit_bytes=16 * 1024 * 1024),
    )(*parts)
    return row_loss.reshape(ROWS), image_grad, text_grad


def solution(mesh):
    rows, wide = P(("group", "blk")), P(("group", "blk"), None)
    return jax.shard_map(
        local,
        mesh=mesh,
        in_specs=(wide, wide, rows, rows, P(), P()),
        out_specs=(rows, wide, wide),
        check_vma=False,
    )
```

```python
import functools

import jax
import jax.numpy as jnp
from jax import lax
from jax.experimental import pallas as pl
from jax.experimental.pallas import tpu as pltpu
from jax.sharding import PartitionSpec as P

MESH = pl.DeviceIdType.MESH
ROWS = 256
D = 1152
N_Z = 8
N_YHI = 4
N_GROUP = 8
STRIP = ROWS // N_Z
CHUNK = 64
N_CHUNK = ROWS // CHUNK
N_EARLY = 3
TILE = 384
F32 = jnp.float32
BF16 = jnp.bfloat16


def rows_of(ref, start, count):
    return ref.at[pl.ds(start, count)]


def backward(raw, inv, grad):
    unit = raw * inv
    return inv * (grad - unit * jnp.sum(unit * grad, axis=-1, keepdims=True))


def kernel(
    images, texts, image_ids, text_ids, log_scale, bias,
    tx, inv_t, image_grad, acc_t, loss_acc,
    im, inv_i, acc_i, ih, th, col_i, col_t, id_rows, ids,
    t1, t2, tg, i1, i2, ig, relay_t, relay_i, ids_in,
    load_sem, id_sem, send_sem, chunk_send, chunk_recv, block_recv, two_recv, pass_send, pass_recv, next_send, prev_send, ids_send, ids_recv, strip_send, ready_next, ready_strip, ready_wrap,
):
    g = lax.axis_index("group")
    k = lax.axis_index("blk")
    core = lax.rem(k, 2)
    z = lax.rem(k // 2, N_Z)
    yhi = k // (2 * N_Z)
    first, last = z == 0, z == N_Z - 1

    def at(yh, zz, cc):
        return (g, (lax.rem(yh + N_YHI, N_YHI) * N_Z + zz) * 2 + cc)

    g_next = (lax.rem(g + 1, N_GROUP), k)
    g_prev = (lax.rem(g + N_GROUP - 1, N_GROUP), k)
    partner = (g, k + 1 - 2 * core)
    wrap_next = at(yhi + 1, 0, core)
    wrap_prev = at(yhi - 1, N_Z - 1, core)
    k_next = (g, lax.rem(k + 2, 2 * N_Z * N_YHI))
    k_prev = (g, lax.rem(k + 2 * N_Z * N_YHI - 2, 2 * N_Z * N_YHI))

    slow = (k == 0) & ((g == 0) | (g == N_GROUP - 1))

    barrier = pltpu.get_barrier_semaphore()

    def tell(device):
        pl.semaphore_signal(barrier, inc=1, device_id=device, device_id_type=MESH)

    tell(g_next)
    tell(g_prev)
    tell(partner)

    loads = []
    id_loads = [
        pltpu.make_async_copy(src, id_rows.at[a], id_sem.at[a])
        for a, src in enumerate((text_ids, image_ids))
    ]
    for a, (src, dst) in enumerate(((texts, tx), (images, im))):
        for c in range(N_CHUNK):
            rows = pl.ds(c * CHUNK, CHUNK)
            copy = pltpu.make_async_copy(src.at[rows], dst.at[rows], load_sem.at[a, c])
            loads.append(copy)
    for copy in loads[:N_CHUNK] + id_loads:
        copy.start()

    @pl.when(jnp.logical_not(last))
    def _():
        tell(k_next)
        tell(at(yhi, N_Z - 1, core))
        tell(wrap_prev)

    @pl.when(last)
    def _():
        tell(at(yhi + 1, N_Z - 1, core))

    @pl.when(first)
    def _():
        tell(wrap_prev)
        for s in range(N_Z - 1):
            tell(at(yhi - 1, s, core))
        for s in range(1, N_Z):
            tell(at(yhi, s, core))

    scale = jnp.exp(jnp.full((1, 1), log_scale[0], F32))
    offset = bias[0]

    def remote(src, dst, send, recv, device):
        return pltpu.make_async_remote_copy(
            src_ref=src, dst_ref=dst, send_sem=send, recv_sem=recv,
            device_id=device, device_id_type=MESH,
        )

    def group_text(c):
        return remote(rows_of(th, c * CHUNK, CHUNK), rows_of(tg, c * CHUNK, CHUNK),
                      chunk_send.at[0, c], chunk_recv.at[0, c], g_next)

    def group_image(c):
        return remote(rows_of(ih, c * CHUNK, CHUNK), rows_of(ig, c * CHUNK, CHUNK),
                      chunk_send.at[1, c], chunk_recv.at[1, c], g_prev)

    def next_text(part):
        return remote(rows_of(th, part * CHUNK, CHUNK), rows_of(t2, part * CHUNK, CHUNK),
                      next_send.at[part], two_recv.at[0, part], k_next)

    def prev_image(part):
        return remote(rows_of(ih, part * CHUNK, CHUNK), rows_of(i2, part * CHUNK, CHUNK),
                      prev_send.at[part], two_recv.at[1, part], k_prev)

    def strip_text(s):
        return remote(rows_of(th, (s + 1) * STRIP, STRIP), relay_t, strip_send.at[s], block_recv.at[2], at(yhi, s, core))

    def strip_image(s):
        return remote(rows_of(ih, s * STRIP, STRIP), relay_i, strip_send.at[s], block_recv.at[3], at(yhi, s, core))

    mine = pl.multiple_of(z * STRIP, STRIP)
    after = pl.multiple_of(lax.rem(z + 1, N_Z) * STRIP, STRIP)
    pass_text = remote(relay_t, rows_of(t2, after, STRIP), send_sem.at[4], two_recv.at[0, after // CHUNK], at(yhi + 1, 0, core))
    pass_image = remote(relay_i, rows_of(i2, mine, STRIP), send_sem.at[5], two_recv.at[1, mine // CHUNK], wrap_prev)
    own_text = remote(rows_of(th, 0, STRIP), rows_of(t2, 0, STRIP), send_sem.at[4], two_recv.at[0, 0], wrap_next)
    own_image = remote(rows_of(ih, 0, STRIP), rows_of(i2, 0, STRIP), send_sem.at[5], two_recv.at[1, 0], wrap_prev)

    core_text = remote(th, t1, send_sem.at[6], block_recv.at[4], partner)
    core_image = remote(ih, i1, send_sem.at[6], block_recv.at[5], partner)

    def on_text(part):
        return remote(rows_of(t2, part * CHUNK, CHUNK), rows_of(t1, part * CHUNK, CHUNK),
                      pass_send.at[part], pass_recv.at[part], partner)

    def on_image(part):
        return remote(rows_of(i2, part * CHUNK, CHUNK), rows_of(i1, part * CHUNK, CHUNK),
                      pass_send.at[part], pass_recv.at[part], partner)

    def send_ids(slot, device, src=ids):
        return remote(src, ids_in.at[slot], ids_send.at[slot], ids_recv.at[slot], device)

    ids_next, ids_prev = send_ids(2, k_next), send_ids(3, k_prev)
    ids_copies = [send_ids(0, g_next), send_ids(1, g_prev), send_ids(4, partner)]
    ids_on_text = send_ids(5, partner, ids_in.at[2])
    ids_on_image = send_ids(5, partner, ids_in.at[3])

    def normalize(c, raw, half_ref, inv_ref):
        rows = pl.ds(c * CHUNK, CHUNK)
        values = raw[rows, :]
        inv = lax.rsqrt(jnp.sum(values * values, axis=-1, keepdims=True) + 1e-06)
        half_ref[rows, :] = (values * inv).astype(BF16)
        inv_ref[rows, :] = jnp.broadcast_to(inv, (CHUNK, 128))

    for c in range(N_CHUNK):
        loads[c].wait()
        if c == 0:
            for copy in loads[N_CHUNK:]:
                copy.start()
        normalize(c, tx, th, inv_t)
        if c == 0:
            pl.semaphore_wait(
                barrier, 4 + 2 * (z > 0).astype(jnp.int32) + 15 * last.astype(jnp.int32)
            )

        @pl.when(last)
        def _():
            if c == 0:
                own_text.start()
            for r in range(c * CHUNK // STRIP, (c + 1) * CHUNK // STRIP):
                if r > 0:
                    strip_text(r - 1).start()

        group_text(c).start()
        if c == 0:
            @pl.when(z > 0)
            def _():
                pl.semaphore_signal(ready_next, inc=1, device_id=k_prev, device_id_type=MESH)
                pl.semaphore_signal(ready_strip.at[z], inc=1, device_id=at(yhi, 0, core), device_id_type=MESH)

            @pl.when(last)
            def _():
                for s in range(N_Z - 1):
                    pl.semaphore_signal(ready_wrap, inc=1, device_id=at(yhi + 1, s, core), device_id_type=MESH)

    @pl.when(core == 0)
    def _():
        core_text.start()

    @pl.when(jnp.logical_not(last))
    def _():
        pl.semaphore_wait(ready_next, 1)
        next_text(0).start()
        next_text(1).start()

    @pl.when(jnp.logical_not(last) & (z > 0))
    def _():
        next_text(2).start()
        next_text(3).start()

    for c in range(N_CHUNK):
        loads[N_CHUNK + c].wait()
        normalize(c, im, ih, inv_i)
        pl.when(z > 0)(prev_image(c).start)

    @pl.when(core == 1)
    def _():
        core_image.start()

    for copy in id_loads:
        copy.wait()
    ids[...] = jnp.concatenate(
        [id_rows[0], id_rows[1], jnp.zeros((6, ROWS), jnp.int32)], axis=0
    )
    col_t[...] = jnp.broadcast_to(id_rows[0].astype(F32), (128, ROWS)).T
    col_i[...] = jnp.broadcast_to(id_rows[1].astype(F32), (128, ROWS)).T
    for copy in ids_copies:
        copy.start()

    ids_next.start()
    pl.when(z > 0)(ids_prev.start)

    def side(own_half, own_col, other, start, count, other_ids, acc, loss, fresh=False):
        block = other[pl.ds(start, count), :]
        dots = lax.dot_general(
            own_half[...], block, (((1,), (1,)), ((), ())), preferred_element_type=F32
        )
        logit = scale * dots + offset
        same = own_col[:, 0:1] == other_ids.astype(F32)
        u = jnp.where(same, -logit, logit)
        e = jnp.exp(-jnp.abs(u))
        coeff = jnp.where(same, -scale, scale) * (jnp.where(u >= 0, 1.0, e) / (1.0 + e))
        coeff = coeff.astype(BF16)
        if loss is not None:
            terms = jnp.maximum(u, 0.0) + jnp.log1p(e)
            terms = jnp.sum(terms, axis=1, keepdims=True)
            terms = jnp.broadcast_to(terms, (ROWS, 128))
            loss[...] = terms if fresh else loss[...] + terms

        for t in range(0, D, TILE):
            cols = pl.ds(t, TILE)
            term = jnp.dot(coeff, other[pl.ds(start, count), cols], preferred_element_type=F32)
            acc[:, cols] = term if fresh else acc[:, cols] + term

    def image_side(block, text_row, start=0, count=ROWS, fresh=False):
        side(ih, col_i, block, start, count, text_row, acc_i, loss_acc, fresh)

    def text_side(block, image_row, start=0, count=ROWS, fresh=False):
        side(th, col_t, block, start, count, image_row, acc_t, None, fresh)

    image_side(th, ids[0:1, :], fresh=True)

    @pl.when(first)
    def _():
        for s in range(1, 5):
            pl.semaphore_wait(ready_strip.at[s], 1)
            strip_image(s).start()
        next_text(2).start()
        next_text(3).start()

    text_side(ih, ids[1:2, :], fresh=True)

    send_ids(4, partner).wait_recv()

    @pl.when(core == 0)
    def _():
        core_image.wait_recv()
        text_side(i1, ids_in[4, 1:2, :])

    @pl.when(core == 1)
    def _():
        core_text.wait_recv()
        image_side(t1, ids_in[4, 0:1, :])

    @pl.when(first)
    def _():
        for s in range(5, N_Z):
            pl.semaphore_wait(ready_strip.at[s], 1)
            strip_image(s).start()

    @pl.when((z >= N_EARLY) & jnp.logical_not(last))
    def _():
        strip_text(0).wait_recv()
        pass_text.start()

    @pl.when(jnp.logical_not(slow))
    def _():
        for c in range(N_CHUNK - 1):
            group_text(c).wait_send()

    group_image(0).start()

    @pl.when(z < N_EARLY)
    def _():
        strip_text(0).wait_recv()
        pass_text.start()

    group_image(1).start()

    def relay_image():
        @pl.when(z > 0)
        def _():
            strip_image(0).wait_recv()

        @pl.when(jnp.logical_not(last))
        def _():
            pl.semaphore_wait(ready_wrap, 1)

        pl.when(z > 0)(pass_image.start)

        @pl.when(first)
        def _():
            own_image.start()
            ids_prev.start()

        for c in range(2, N_CHUNK):
            group_image(c).start()

    def meet_image():
        ids_prev.wait_recv()
        pl.when(core == 0)(ids_on_image.start)
        for part in range(N_CHUNK):
            prev_image(part).wait_recv()
            pl.when(core == 0)(on_image(part).start)
        text_side(i2, ids_in[3, 1:2, :])

    def meet_text():
        ids_next.wait_recv()
        pl.when(core == 1)(ids_on_text.start)
        for part in range(N_CHUNK):
            next_text(part).wait_recv()
            pl.when(core == 1)(on_text(part).start)
        image_side(t2, ids_in[2, 0:1, :])

    def meet_passed_text():
        ids_on_text.wait_recv()
        for part in range(N_CHUNK):
            on_text(part).wait_recv()
        image_side(t1, ids_in[5, 0:1, :])

    def meet_passed_image():
        ids_on_image.wait_recv()
        for part in range(N_CHUNK):
            on_image(part).wait_recv()
        text_side(i1, ids_in[5, 1:2, :])

    pl.when((z < 2) | (z >= 6))(relay_image)
    pl.when(jnp.logical_not(first))(meet_text)
    pl.when((z >= 2) & (z < 6))(relay_image)
    pl.when(jnp.logical_not(last))(meet_image)
    pl.when(jnp.logical_not(last) & (core == 1))(meet_passed_image)
    pl.when(jnp.logical_not(first) & (core == 0))(meet_passed_text)

    ids_copies[0].wait_recv()
    ids_copies[1].wait_recv()
    for c in range(N_CHUNK):
        group_text(c).wait_recv()
    image_side(tg, ids_in[0, 0:1, :])

    def meet_group_image(begin, stop):
        here, count = begin * CHUNK, (stop - begin) * CHUNK
        for c in range(begin, stop):
            group_image(c).wait_recv()
        text_side(ig, ids_in[1, 1:2, here:here + count], here, count)

    def image_backward():
        for c in range(N_CHUNK):
            rows = pl.ds(c * CHUNK, CHUNK)
            image_grad[rows, :] = backward(im[rows, :], inv_i[rows, 0:1], acc_i[rows, :])

    pl.when(jnp.logical_not(first))(image_backward)
    pl.when(last & (core == 0))(meet_image)
    meet_group_image(0, N_CHUNK - 1)
    pl.when(first & (core == 1))(meet_text)
    pl.when(first & (core == 0))(meet_passed_text)
    pl.when(last & (core == 1))(meet_image)
    pl.when(last & (core == 1))(meet_passed_image)
    meet_group_image(N_CHUNK - 1, N_CHUNK)
    pl.when(first & (core == 0))(meet_text)
    pl.when(first)(image_backward)

    @pl.when(slow)
    def _():
        for c in range(N_CHUNK - 1):
            group_text(c).wait_send()

    group_text(N_CHUNK - 1).wait_send()
    for c in range(N_CHUNK):
        group_image(c).wait_send()
    for copy in ids_copies:
        copy.wait_send()
    ids_next.wait_send()
    ids_prev.wait_send()
    ids_on_text.wait_send()
    core_text.wait_send()
    for part in range(N_CHUNK):
        on_text(part).wait_send()

    @pl.when(z > 0)
    def _():
        for part in range(N_CHUNK):
            prev_image(part).wait_send()

    @pl.when(jnp.logical_not(last))
    def _():
        for part in range(N_CHUNK):
            next_text(part).wait_send()

    pass_text.wait_send()
    pass_image.wait_send()

    @pl.when(last)
    def _():
        for s in range(N_Z - 1):
            strip_text(s).wait_send()

    @pl.when(first)
    def _():
        for s in range(1, N_Z):
            strip_image(s).wait_send()


def finish(tx, inv_t, image_grad, acc_t, loss_acc, loss_out, image_out, text_out, row, buf, sems):
    image_copy = pltpu.make_async_copy(image_grad, image_out, sems.at[N_CHUNK])
    image_copy.start()
    copies = [image_copy]
    for c in range(N_CHUNK):
        rows = pl.ds(c * CHUNK, CHUNK)
        buf[rows, :] = backward(tx[rows, :], inv_t[rows, 0:1], acc_t[rows, :])
        copy = pltpu.make_async_copy(buf.at[rows], text_out.at[rows], sems.at[c])
        copy.start()
        copies.append(copy)
    row[...] = loss_acc[...].T[0:1, :]
    loss_copy = pltpu.make_async_copy(row, loss_out, sems.at[N_CHUNK + 1])
    loss_copy.start()
    for copy in copies + [loss_copy]:
        copy.wait()


def local(images, texts, image_ids, text_ids, log_scale, bias):
    block = pltpu.VMEM((ROWS, D), BF16)
    wide = pltpu.VMEM((ROWS, D), F32)
    lanes = pltpu.VMEM((ROWS, 128), F32)
    wide_out = jax.ShapeDtypeStruct((ROWS, D), F32)
    lanes_out = jax.ShapeDtypeStruct((ROWS, 128), F32)
    dma, plain = pltpu.SemaphoreType.DMA, pltpu.SemaphoreType.REGULAR
    vmem = pl.BlockSpec(memory_space=pltpu.VMEM)
    smem = pl.BlockSpec(memory_space=pltpu.SMEM)
    hbm = pl.BlockSpec(memory_space=pltpu.HBM)
    given = (images, texts, image_ids.reshape(1, ROWS), text_ids.reshape(1, ROWS))
    in_hbm = [pltpu.with_memory_space_constraint(a, pltpu.HBM) for a in given]
    parts = pl.pallas_call(
        kernel,
        out_shape=(wide_out, lanes_out, wide_out, wide_out, lanes_out),
        in_specs=[hbm, hbm, hbm, hbm, smem, smem],
        out_specs=(vmem,) * 5,
        scratch_shapes=[
            wide, lanes, wide, block, block, lanes, lanes, pltpu.VMEM((2, 1, ROWS), jnp.int32),
            pltpu.VMEM((8, ROWS), jnp.int32),
            block, block, block, block, block, block,
            pltpu.VMEM((STRIP, D), BF16), pltpu.VMEM((STRIP, D), BF16),
            pltpu.VMEM((6, 8, ROWS), jnp.int32),
            dma((2, N_CHUNK)), dma((2,)), dma((8,)), dma((2, N_CHUNK)), dma((2, N_CHUNK)), dma((6,)),
            dma((2, N_CHUNK)), dma((N_CHUNK,)), dma((N_CHUNK,)), dma((N_CHUNK,)), dma((N_CHUNK,)), dma((6,)), dma((6,)), dma((N_Z,)), plain, plain((N_Z,)), plain,
        ],
        compiler_params=pltpu.CompilerParams(
            collective_id=0, has_side_effects=True, vmem_limit_bytes=32 * 1024 * 1024
        ),
    )(*in_hbm, log_scale, bias)
    row_loss, image_grad, text_grad = pl.pallas_call(
        finish,
        out_shape=(jax.ShapeDtypeStruct((1, ROWS), F32), wide_out, wide_out),
        in_specs=[vmem] * 5,
        out_specs=(hbm,) * 3,
        scratch_shapes=[pltpu.VMEM((1, ROWS), F32), wide, dma((N_CHUNK + 2,))],
        compiler_params=pltpu.CompilerParams(vmem_limit_bytes=16 * 1024 * 1024),
    )(*parts)
    return row_loss.reshape(ROWS), image_grad, text_grad


def solution(mesh):
    rows, wide = P(("group", "blk")), P(("group", "blk"), None)
    return jax.shard_map(
        local,
        mesh=mesh,
        in_specs=(wide, wide, rows, rows, P(), P()),
        out_specs=(rows, wide, wide),
        check_vma=False,
    )
```
